512 devices in a mesh: replica: 32 (over x, y, z_hi), fsdp: 16 (over z_lo, core).
Axes of the slice: x: 4, y: 4, z: 16 (z_hi: 2, z_lo: 8; z = z_hi * 8 + z_lo), core: 2. Of those that a mesh axis runs over, the one named last changes fastest.
Arguments:
- tokens: bfloat16 [98304, 4096], P(('replica', 'fsdp')), may hold values from -6 to 6
- grads_out: bfloat16 [98304, 1024], P(('replica', 'fsdp')), may hold values from -6 to 6
- weights: bfloat16 [32, 4096, 1024], P('replica', 'fsdp'), may hold values from -0.29882812 to 0.29882812
- moments: float32 [32, 4096, 1024], P('replica', 'fsdp'), may hold values from -6 to 6
- step: int32 [1], replicated, may hold values from 0 to 999
Outputs:
- mixed_weights: bfloat16 [32, 4096, 1024], P('replica', 'fsdp')
- new_moments: float32 [32, 4096, 1024], P('replica', 'fsdp')
The draws below stay inside these ranges and needn't reach their ends.
All inputs are finite; a program needn't handle non-finite values.
Results may differ from the reference program's by a relative error of at most 0.001.
Values may be sent and summed in bfloat16 or wider, within the bound.
A program may use at most 64 MiB of HBM per device.

```python
import jax
import jax.numpy as jnp
from jax import lax

D = 4096
C = 1024
TOKENS = 3072
ROWS = 98304
N_REPLICA = 32


def block_scale(key, extent, split, low, largest):
    factor_of = 1.0
    for dim, parts in split:
        draws = jax.random.uniform(jax.random.fold_in(jax.random.fold_in(key, 6), dim), (parts,), jnp.float32, low / len(split), largest / len(split))
        factor_of = factor_of * jnp.repeat(jnp.exp(draws), extent[dim] // parts).reshape((-1,) + (1,) * (len(extent) - 1 - dim))
    return factor_of


def gaussian(rng, extent, spread, reach, shards=(), held_as=jnp.bfloat16):
    entries = spread * jax.random.normal(rng, extent, jnp.float32)
    if shards:
        entries = entries * block_scale(rng, extent, shards, -0.22, 0.18)
    return jnp.clip(entries, -reach, reach).astype(held_as)


def setup_inputs(seed: int = 0) -> dict:
    streams_of = jax.random.split(jax.random.key(seed), 6)
    tokens = gaussian(streams_of[0], (ROWS, D), 1.0, 6.0, ((0, 512),))
    grads_out = gaussian(streams_of[1], (ROWS, C), 1.0, 6.0, ((0, 512),))
    weights = gaussian(streams_of[2], (N_REPLICA, D, C), 0.05, 0.29882812, ((0, 32), (1, 16)))
    moments = gaussian(streams_of[3], (N_REPLICA, D, C), 1.0, 6.0, ((0, 32), (1, 16)), jnp.float32)
    step = jax.random.randint(streams_of[4], (1,), 0, 1000).astype(jnp.int32)
    return dict(tokens=tokens, grads_out=grads_out, weights=weights, moments=moments, step=step)


def one_replica(pair):
    inputs, cotangent = pair
    return jnp.dot(inputs.T, cotangent, preferred_element_type=jnp.float32)


def reference(tokens, grads_out, weights, moments, step):
    inputs = tokens.reshape(N_REPLICA, TOKENS, D)
    cotangent = grads_out.reshape(N_REPLICA, TOKENS, C)
    gradient = lax.map(one_replica, (inputs, cotangent)) * jnp.float32(TOKENS ** -0.5)
    new_moments = 0.9 * moments + gradient
    updated = weights.astype(jnp.float32) - 0.05 * new_moments
    levels = N_REPLICA.bit_length() - 1
    level = (step[0] % levels).astype(jnp.int32)
    distance = jnp.left_shift(jnp.int32(1), level)
    partner = jnp.roll(updated, distance, axis=0)
    mixed_weights = ((updated + partner) * 0.5).astype(jnp.bfloat16)
    return mixed_weights, new_moments
```

```python
import functools

import jax
import jax.numpy as jnp
from jax import lax
from jax.experimental import pallas as pl
from jax.experimental.pallas import tpu as pltpu
from jax.sharding import PartitionSpec as P

MESH = pl.DeviceIdType.MESH
TOP = 32767.0
TINY = 1e-30
UNITS = 4
HOP = 2
LANES = 256


def kernel(
    replicas,
    chips,
    distance,
    scale,
    tokens_hbm,
    grads_hbm,
    weights_hbm,
    moments_hbm,
    mixed_hbm,
    new_hbm,
    tok,
    grad,
    buf,
    factor,
    part,
    weights,
    moments,
    new,
    updated,
    mixed,
    out_buf,
    out_factor,
    in_buf,
    in_factor,
    own_sem,
    sib_send,
    sib_recv,
    load_sem,
    send,
    recv,
    factor_send,
    factor_recv,
    gossip_send,
    gossip_recv,
    gossip_factor_send,
    gossip_factor_recv,
    new_sem,
    mixed_sem,
):
    last = chips - 1
    features, columns = updated.shape
    rows = features // UNITS
    width = min(LANES, columns)
    replica = lax.axis_index("replica")
    me = lax.axis_index("fsdp")
    chip = me // 2
    core = me % 2
    sibling = chip * 2 + 1 - core
    left = jnp.maximum(me - 2, 0)
    right = jnp.minimum(me + 2, 2 * chips - 1)
    partner = (replica + distance) % replicas
    source = (replica + replicas - distance) % replicas

    def piece(target, which):
        start = pl.multiple_of((2 * target + which) * features, features)
        return tokens_hbm.at[:, pl.ds(start, features)]

    def own_copy(target):
        return pltpu.make_async_copy(
            piece(target, core), tok.at[target, core], own_sem.at[target]
        )

    def sibling_copy(target):
        return pltpu.make_async_remote_copy(
            src_ref=piece(target, 1 - core),
            dst_ref=tok.at[target, core],
            send_sem=sib_send.at[target],
            recv_sem=sib_recv.at[target],
            device_id={"fsdp": sibling},
            device_id_type=MESH,
        )

    own_grad = pltpu.make_async_copy(grads_hbm, grad.at[core], own_sem.at[chips])
    sibling_grad = pltpu.make_async_remote_copy(
        src_ref=grads_hbm,
        dst_ref=grad.at[core],
        send_sem=sib_send.at[chips],
        recv_sem=sib_recv.at[chips],
        device_id={"fsdp": sibling},
        device_id_type=MESH,
    )
    load_weights = pltpu.make_async_copy(weights_hbm.at[0], weights, load_sem.at[0])
    load_moments = pltpu.make_async_copy(moments_hbm.at[0], moments, load_sem.at[1])

    order = []
    for near in range(chips // 2):
        order += [near, last - near]

    barrier = pltpu.get_barrier_semaphore()
    pl.semaphore_signal(barrier, inc=1, device_id={"fsdp": sibling}, device_id_type=MESH)
    pl.semaphore_signal(barrier, inc=1, device_id={"replica": source}, device_id_type=MESH)

    @pl.when(chip > 0)
    def _():
        pl.semaphore_signal(barrier, inc=1, device_id={"fsdp": left}, device_id_type=MESH)

    @pl.when(chip < last)
    def _():
        pl.semaphore_signal(barrier, inc=1, device_id={"fsdp": right}, device_id_type=MESH)

    own_grad.start()
    for target in order:
        own_copy(target).start()
    load_weights.start()
    load_moments.start()

    pl.semaphore_wait(
        barrier, 2 + (chip > 0).astype(jnp.int32) + (chip < last).astype(jnp.int32)
    )

    sibling_grad.start()
    for target in order:
        sibling_copy(target).start()
    own_grad.wait()
    sibling_grad.wait_recv()

    def multiply(target, slot):
        own_copy(target).wait()
        sibling_copy(target).wait_recv()
        left_side = tok[target].reshape(-1, features)
        right_side = grad[...].reshape(-1, columns)
        part[slot] = lax.dot_general(
            left_side,
            right_side,
            (((0,), (0,)), ((), ())),
            preferred_element_type=jnp.float32,
        )

    def hop(way, unit):
        to = left if way == 0 else right
        data = pltpu.make_async_remote_copy(
            src_ref=buf.at[way, unit],
            dst_ref=buf.at[way, unit],
            send_sem=send.at[way, unit],
            recv_sem=recv.at[way, unit],
            device_id={"fsdp": to},
            device_id_type=MESH,
        )
        factors = pltpu.make_async_remote_copy(
            src_ref=factor.at[way, unit],
            dst_ref=factor.at[way, unit],
            send_sem=factor_send.at[way, unit],
            recv_sem=factor_recv.at[way, unit],
            device_id={"fsdp": to},
            device_id_type=MESH,
        )
        return data, factors

    def gossip(unit):
        data = pltpu.make_async_remote_copy(
            src_ref=out_buf.at[unit],
            dst_ref=in_buf.at[unit],
            send_sem=gossip_send.at[unit],
            recv_sem=gossip_recv.at[unit],
            device_id={"replica": partner},
            device_id_type=MESH,
        )
        factors = pltpu.make_async_remote_copy(
            src_ref=out_factor.at[unit],
            dst_ref=in_factor.at[unit],
            send_sem=gossip_factor_send.at[unit],
            recv_sem=gossip_factor_recv.at[unit],
            device_id={"replica": partner},
            device_id_type=MESH,
        )
        return data, factors

    def new_copy(unit):
        at = pl.ds(pl.multiple_of(unit * rows, rows), rows)
        return pltpu.make_async_copy(new.at[at], new_hbm.at[0, at], new_sem.at[unit])

    def mixed_copy(unit):
        at = pl.ds(pl.multiple_of(unit * rows, rows), rows)
        return pltpu.make_async_copy(mixed.at[at], mixed_hbm.at[0, at], mixed_sem.at[unit])

    def decode(data, factors):
        return data.astype(jnp.int32).astype(jnp.float32) * factors

    def encode(value):
        largest = jnp.max(jnp.abs(value), axis=0, keepdims=True)
        largest = jnp.maximum(largest, TINY)
        code = jnp.round(value * (TOP / largest * (1.0 - 1e-6)))
        return code.astype(jnp.int32).astype(jnp.int16), largest * (1.0 / TOP / (1.0 - 1e-6))

    def forward(way, unit, target, has_upstream):
        index = unit % UNITS

        @pl.when(index == 0)
        def _():
            multiply(target, way)

        @pl.when(has_upstream)
        def _():
            for copy in hop(way, unit):
                copy.wait_recv()

        at = pl.ds(pl.multiple_of(index * rows, rows), rows)

        @pl.when(has_upstream)
        def _():
            for begin in range(0, columns, width):
                cut = slice(begin, begin + width)
                value = part[way, at, cut] + decode(buf[way, unit, :, cut], factor[way, unit, :, cut])
                buf[way, unit, :, cut], factor[way, unit, :, cut] = encode(value)

        @pl.when(jnp.logical_not(has_upstream))
        def _():
            for begin in range(0, columns, width):
                cut = slice(begin, begin + width)
                buf[way, unit, :, cut], factor[way, unit, :, cut] = encode(part[way, at, cut])

        for copy in hop(way, unit):
            copy.start()

    from_right = chip * UNITS
    from_left = (last - chip) * UNITS
    lag_right = (last - chip) * HOP
    lag_left = chip * HOP

    def finish(unit):
        @pl.when(unit == 0)
        def _():
            multiply(chip, 2)
            load_weights.wait()
            load_moments.wait()

        at = pl.ds(pl.multiple_of(unit * rows, rows), rows)

        for way, begin_unit, there in ((0, from_right, chip < last), (1, from_left, chip > 0)):

            @pl.when(there)
            def _(way=way, begin_unit=begin_unit):
                arrived = jnp.minimum(begin_unit, last * UNITS - UNITS) + unit
                for copy in hop(way, arrived):
                    copy.wait_recv()
                for begin in range(0, columns, width):
                    cut = slice(begin, begin + width)
                    part[2, at, cut] += decode(
                        buf[way, arrived, :, cut], factor[way, arrived, :, cut]
                    )

        for begin in range(0, columns, width):
            cut = slice(begin, begin + width)
            moment = 0.9 * moments[at, cut] + part[2, at, cut] * scale
            new[at, cut] = moment
            value = weights[at, cut].astype(jnp.float32) - 0.05 * moment
            updated[at, cut] = value
            out_buf[unit, :, cut], out_factor[unit, :, cut] = encode(value)
        for copy in gossip(unit):
            copy.start()
        new_copy(unit).start()

    begin_finish = jnp.maximum(
        jnp.where(chip < last, from_right + lag_right, 0),
        jnp.where(chip > 0, from_left + lag_left, 0),
    )

    def step(i, carry):
        unit_l = i - lag_right
        unit_r = i - lag_left
        unit_o = i - begin_finish

        @pl.when(jnp.logical_and(unit_l >= 0, unit_l < from_right))
        def _():
            forward(0, unit_l, unit_l // UNITS, chip < last)

        @pl.when(jnp.logical_and(unit_r >= 0, unit_r < from_left))
        def _():
            forward(1, unit_r, last - unit_r // UNITS, chip > 0)

        @pl.when(jnp.logical_and(unit_o >= 0, unit_o < UNITS))
        def _():
            finish(unit_o)

        return carry

    steps = last * max(UNITS, HOP) + UNITS + HOP
    lax.fori_loop(0, steps, step, 0)

    def mix(unit, carry):
        for copy in gossip(unit):
            copy.wait_recv()
        at = pl.ds(pl.multiple_of(unit * rows, rows), rows)
        for begin in range(0, columns, width):
            cut = slice(begin, begin + width)
            theirs = decode(in_buf[unit, :, cut], in_factor[unit, :, cut])
            mixed[at, cut] = ((updated[at, cut] + theirs) * 0.5).astype(jnp.bfloat16)
        mixed_copy(unit).start()
        return carry

    lax.fori_loop(0, UNITS, mix, 0)

    def drain_left(unit, carry):
        for copy in hop(0, unit):
            copy.wait_send()
        return carry

    def drain_right(unit, carry):
        for copy in hop(1, unit):
            copy.wait_send()
        return carry

    lax.fori_loop(0, from_right, drain_left, 0)
    lax.fori_loop(0, from_left, drain_right, 0)
    sibling_grad.wait_send()
    for target in range(chips):
        sibling_copy(target).wait_send()

    def drain(unit, carry):
        for copy in gossip(unit):
            copy.wait_send()
        new_copy(unit).wait()
        mixed_copy(unit).wait()
        return carry

    lax.fori_loop(0, UNITS, drain, 0)


def step_with(level, replicas, members, tokens, grads_out, weights, moments):
    chips = members // 2
    held, features_all = tokens.shape
    columns = grads_out.shape[1]
    features = weights.shape[1]
    rows = features // UNITS
    passed = (chips - 1) * UNITS
    dma = pltpu.SemaphoreType.DMA
    return pl.pallas_call(
        functools.partial(
            kernel, replicas, chips, 1 << level, float((held * members) ** -0.5)
        ),
        out_shape=(
            jax.ShapeDtypeStruct(weights.shape, jnp.bfloat16),
            jax.ShapeDtypeStruct(moments.shape, jnp.float32),
        ),
        in_specs=[pl.BlockSpec(memory_space=pl.ANY)] * 4,
        out_specs=[pl.BlockSpec(memory_space=pl.ANY)] * 2,
        scratch_shapes=[
            pltpu.VMEM((chips, 2, held, features), jnp.bfloat16),
            pltpu.VMEM((2, held, columns), jnp.bfloat16),
            pltpu.VMEM((2, passed, rows, columns), jnp.int16),
            pltpu.VMEM((2, passed, 1, columns), jnp.float32),
            pltpu.VMEM((3, features, columns), jnp.float32),
            pltpu.VMEM((features, columns), jnp.bfloat16),
            pltpu.VMEM((features, columns), jnp.float32),
            pltpu.VMEM((features, columns), jnp.float32),
            pltpu.VMEM((features, columns), jnp.float32),
            pltpu.VMEM((features, columns), jnp.bfloat16),
            pltpu.VMEM((UNITS, rows, columns), jnp.int16),
            pltpu.VMEM((UNITS, 1, columns), jnp.float32),
            pltpu.VMEM((UNITS, rows, columns), jnp.int16),
            pltpu.VMEM((UNITS, 1, columns), jnp.float32),
            dma((chips + 1,)),
            dma((chips + 1,)),
            dma((chips + 1,)),
            dma((2,)),
            dma((2, passed)),
            dma((2, passed)),
            dma((2, passed)),
            dma((2, passed)),
            dma((UNITS,)),
            dma((UNITS,)),
            dma((UNITS,)),
            dma((UNITS,)),
            dma((UNITS,)),
            dma((UNITS,)),
        ],
        compiler_params=pltpu.CompilerParams(
            collective_id=level, has_side_effects=True, vmem_limit_bytes=44 * 1024 * 1024
        ),
        cost_estimate=pl.CostEstimate(
            flops=2 * held * members * features * columns,
            bytes_accessed=2 * tokens.size + 10 * features * columns,
            transcendentals=0,
        ),
    )(tokens, grads_out, weights, moments)


def solution(mesh):
    replicas, members = mesh.shape["replica"], mesh.shape["fsdp"]
    levels = replicas.bit_length() - 1

    def body(tokens, grads_out, weights, moments, step):
        level = step[0] % levels
        branches = [
            functools.partial(step_with, power, replicas, members) for power in range(levels)
        ]
        return lax.switch(level, branches, tokens, grads_out, weights, moments)

    return jax.shard_map(
        body,
        mesh=mesh,
        in_specs=(
            P(("replica", "fsdp"), None),
            P(("replica", "fsdp"), None),
            P("replica", "fsdp", None),
            P("replica", "fsdp", None),
            P(),
        ),
        out_specs=(P("replica", "fsdp", None), P("replica", "fsdp", None)),
        check_vma=False,
    )
```

```python
import functools

import jax
import jax.numpy as jnp
from jax import lax
from jax.experimental import pallas as pl
from jax.experimental.pallas import tpu as pltpu
from jax.sharding import PartitionSpec as P

MESH = pl.DeviceIdType.MESH
TOP = 32767.0
TINY = 1e-30
HOP = 2
LANES = 256
GROUP = 64


def kernel(
    replicas,
    chips,
    distance,
    scale,
    tokens_hbm,
    grads_hbm,
    weights_hbm,
    moments_hbm,
    mixed_hbm,
    new_hbm,
    tok,
    grad,
    edge_tok,
    edge_grad,
    buf,
    factor,
    part,
    weights,
    moments,
    new,
    updated,
    mixed,
    out_buf,
    out_factor,
    in_buf,
    in_factor,
    own_sem,
    sib_send,
    sib_recv,
    own_grad_sem,
    sib_grad_send,
    sib_grad_recv,
    load_sem,
    edge_send,
    edge_recv,
    edge_grad_send,
    edge_grad_recv,
    pass_send,
    pass_recv,
    send,
    recv,
    factor_send,
    factor_recv,
    gossip_send,
    gossip_recv,
    gossip_factor_send,
    gossip_factor_recv,
    new_sem,
    mixed_sem,
):
    last = chips - 1
    units, features, width = updated.shape
    replica = lax.axis_index("replica")
    me = lax.axis_index("fsdp")
    chip = me // 2
    core = me % 2
    sibling = chip * 2 + 1 - core
    left = jnp.maximum(me - 2, 0)
    right = jnp.minimum(me + 2, 2 * chips - 1)
    partner = (replica + distance) % replicas
    source = (replica + replicas - distance) % replicas
    at_end = jnp.logical_or(chip == 0, chip == last)
    next_to_end = jnp.logical_or(chip == 1, chip == last - 1)
    high = chip >= chips // 2
    inner = jnp.where(high, last - 1, 1)
    outer = jnp.where(high, last, 0)

    def span(unit):
        return pl.ds(pl.multiple_of(unit * width, width), width)

    def remote(source_ref, to_ref, send_sem, recv_sem, device):
        return pltpu.make_async_remote_copy(
            src_ref=source_ref,
            dst_ref=to_ref,
            send_sem=send_sem,
            recv_sem=recv_sem,
            device_id=device,
            device_id_type=MESH,
        )

    def piece(target, which):
        start = pl.multiple_of((2 * target + which) * features, features)
        return tokens_hbm.at[:, pl.ds(start, features)]

    def own_copy(target):
        return pltpu.make_async_copy(piece(target, core), tok.at[target, core], own_sem.at[target])

    def sibling_copy(target):
        return remote(
            piece(target, 1 - core),
            tok.at[target, core],
            sib_send.at[target],
            sib_recv.at[target],
            {"fsdp": sibling},
        )

    def own_grad(unit):
        return pltpu.make_async_copy(
            grads_hbm.at[:, span(unit)], grad.at[unit, core], own_grad_sem.at[unit]
        )

    def sibling_grad(unit):
        return remote(
            grads_hbm.at[:, span(unit)],
            grad.at[unit, core],
            sib_grad_send.at[unit],
            sib_grad_recv.at[unit],
            {"fsdp": sibling},
        )

    def edge_target(rank):
        return jnp.where(high, rank, last - rank)

    def edge_copy(rank, which):
        return remote(
            piece(edge_target(rank), which),
            edge_tok.at[rank, core],
            edge_send.at[rank, which],
            edge_recv.at[rank, core],
            {"fsdp": inner * 2 + which},
        )

    def edge_arrival(rank, which):
        return remote(
            edge_tok.at[rank, which],
            edge_tok.at[rank, which],
            edge_send.at[rank, which],
            edge_recv.at[rank, which],
            {"fsdp": sibling},
        )

    def edge_grad_copy(unit):
        return remote(
            grads_hbm.at[:, span(unit)],
            edge_grad.at[unit, core],
            edge_grad_send.at[unit],
            edge_grad_recv.at[unit],
            {"fsdp": inner * 2 + core},
        )

    def edge_grad_arrival(unit):
        return remote(
            edge_grad.at[unit, core],
            edge_grad.at[unit, core],
            edge_grad_send.at[unit],
            edge_grad_recv.at[unit],
            {"fsdp": sibling},
        )

    def pass_copy(unit, which):
        return remote(
            edge_grad.at[unit, which],
            edge_grad.at[unit, which],
            pass_send.at[unit],
            pass_recv.at[unit],
            {"fsdp": sibling},
        )

    def load(unit):
        return (
            pltpu.make_async_copy(
                weights_hbm.at[0, :, span(unit)], weights.at[unit], load_sem.at[0, unit]
            ),
            pltpu.make_async_copy(
                moments_hbm.at[0, :, span(unit)], moments.at[unit], load_sem.at[1, unit]
            ),
        )

    def hop(way, slot):
        device = {"fsdp": left if way == 0 else right}
        return (
            remote(
                buf.at[way, slot],
                buf.at[way, slot],
                send.at[way, slot],
                recv.at[way, slot],
                device,
            ),
            remote(
                factor.at[way, slot],
                factor.at[way, slot],
                factor_send.at[way, slot],
                factor_recv.at[way, slot],
                device,
            ),
        )

    def gossip(unit):
        device = {"replica": partner}
        return (
            remote(
                out_buf.at[unit],
                in_buf.at[unit],
                gossip_send.at[unit],
                gossip_recv.at[unit],
                device,
            ),
            remote(
                out_factor.at[unit],
                in_factor.at[unit],
                gossip_factor_send.at[unit],
                gossip_factor_recv.at[unit],
                device,
            ),
        )

    def new_copy(unit):
        return pltpu.make_async_copy(new.at[unit], new_hbm.at[0, :, span(unit)], new_sem.at[unit])

    def mixed_copy(unit):
        return pltpu.make_async_copy(
            mixed.at[unit], mixed_hbm.at[0, :, span(unit)], mixed_sem.at[unit]
        )

    order = []
    for near in range(chips // 2):
        order += [near, last - near]

    barrier = pltpu.get_barrier_semaphore()
    pl.semaphore_signal(barrier, inc=1, device_id={"fsdp": sibling}, device_id_type=MESH)
    pl.semaphore_signal(barrier, inc=1, device_id={"replica": source}, device_id_type=MESH)

    @pl.when(chip > 0)
    def _():
        pl.semaphore_signal(barrier, inc=1, device_id={"fsdp": left}, device_id_type=MESH)

    @pl.when(chip < last)
    def _():
        pl.semaphore_signal(barrier, inc=1, device_id={"fsdp": right}, device_id_type=MESH)

    @pl.when(next_to_end)
    def _():
        pl.semaphore_signal(
            barrier, inc=1, device_id={"fsdp": outer * 2 + 1 - core}, device_id_type=MESH
        )

    for unit in range(units):
        own_grad(unit).start()
    def needs(target):
        return jnp.logical_or(jnp.logical_not(at_end), chip == target)

    for target in order:

        @pl.when(needs(target))
        def _(target=target):
            own_copy(target).start()

    pl.semaphore_wait(barrier, 4)

    @pl.when(at_end)
    def _():
        edge_grad_copy(0).start()
        edge_copy(0, 0).start()
        edge_copy(0, 1).start()

    for unit in range(units):
        sibling_grad(unit).start()
    for target in order:

        @pl.when(needs(target))
        def _(target=target):
            sibling_copy(target).start()

    @pl.when(at_end)
    def _():
        for unit in range(1, units):
            edge_grad_copy(unit).start()
        for rank in range(1, last):
            edge_copy(rank, 0).start()
            edge_copy(rank, 1).start()

    for unit in range(units):
        for copy in load(unit):
            copy.start()

    for unit in range(units):
        own_grad(unit).wait()
        sibling_grad(unit).wait_recv()

    def dot(a, b):
        return lax.dot_general(
            a.reshape(-1, a.shape[-1]),
            b.reshape(-1, b.shape[-1]),
            (((0,), (0,)), ((), ())),
            preferred_element_type=jnp.float32,
        )

    def decode(data, factors):
        return data.astype(jnp.int32).astype(jnp.float32) * factors

    def encode(value):
        largest = jnp.max(jnp.abs(value), axis=0, keepdims=True)
        largest = jnp.maximum(largest, TINY)
        code = jnp.round(value * (TOP / largest * (1.0 - 1e-6)))
        return code.astype(jnp.int32).astype(jnp.int16), largest * (1.0 / TOP / (1.0 - 1e-6))

    groups = [(g, slice(g * GROUP, (g + 1) * GROUP)) for g in range(features // GROUP)]

    def multiply(slot, target, rank, unit, with_edge):
        @pl.when(unit == 0)
        def _():
            own_copy(target).wait()
            sibling_copy(target).wait_recv()

        part[slot] = dot(tok[target], grad[unit])

        @pl.when(with_edge)
        def _():
            @pl.when(rank == 0)
            def _():
                edge_grad_arrival(unit).wait_recv()
                pass_copy(unit, core).start()
                pass_copy(unit, 1 - core).wait_recv()

            @pl.when(unit == 0)
            def _():
                edge_arrival(rank, 0).wait_recv()
                edge_arrival(rank, 1).wait_recv()

            part[slot] += dot(edge_tok[rank], edge_grad[unit])

    def receive(slot, way, at):
        for copy in hop(way, at):
            copy.wait_recv()
        for g, rows in groups:
            part[slot, rows] += decode(buf[way, at, rows], factor[way, at, g : g + 1])

    def forward(way, at, beside_end):
        rank = at // units
        multiply(way, rank if way == 0 else last - rank, rank, at % units, beside_end)

        @pl.when(jnp.logical_not(beside_end))
        def _():
            receive(way, way, at)

        for g, rows in groups:
            buf[way, at, rows], factor[way, at, g : g + 1] = encode(part[way, rows])
        for copy in hop(way, at):
            copy.start()

    from_right = chip * units
    from_left = (last - chip) * units
    lag_right = jnp.maximum(last - 1 - chip, 0) * HOP
    lag_left = jnp.maximum(chip - 1, 0) * HOP
    largest_slot = (last - 1) * units - 1

    def finish(unit):
        multiply(2, chip, last - 1, unit, next_to_end)

        @pl.when(chip < last - 1)
        def _():
            receive(2, 0, jnp.minimum(from_right + unit, largest_slot))

        @pl.when(chip > 1)
        def _():
            receive(2, 1, jnp.minimum(from_left + unit, largest_slot))

        for copy in load(unit):
            copy.wait()
        for g, rows in groups:
            moment = 0.9 * moments[unit, rows] + part[2, rows] * scale
            new[unit, rows] = moment
            value = weights[unit, rows].astype(jnp.float32) - 0.05 * moment
            updated[unit, rows] = value
            out_buf[unit, rows], out_factor[unit, g : g + 1] = encode(value)
        for copy in gossip(unit):
            copy.start()
        new_copy(unit).start()

    begin_finish = jnp.maximum(
        jnp.where(chip < last, from_right + lag_right, 0),
        jnp.where(chip > 0, from_left + lag_left, 0),
    )

    def step(i, carry):
        at_l = i - lag_right
        at_r = i - lag_left
        unit = i - begin_finish

        @pl.when((at_l >= 0) & (at_l < from_right) & (chip < last))
        def _():
            forward(0, at_l, chip == last - 1)

        @pl.when((at_r >= 0) & (at_r < from_left) & (chip > 0))
        def _():
            forward(1, at_r, chip == 1)

        @pl.when((unit >= 0) & (unit < units))
        def _():
            finish(unit)

        return carry

    steps = (last - 1) * max(units, HOP) + units + HOP
    lax.fori_loop(0, steps, step, 0)

    def mix(unit, carry):
        for copy in gossip(unit):
            copy.wait_recv()
        for g, rows in groups:
            theirs = decode(in_buf[unit, rows], in_factor[unit, g : g + 1])
            mixed[unit, rows] = ((updated[unit, rows] + theirs) * 0.5).astype(jnp.bfloat16)
        mixed_copy(unit).start()
        return carry

    lax.fori_loop(0, units, mix, 0)

    def drain_left(at, carry):
        for copy in hop(0, at):
            copy.wait_send()
        return carry

    def drain_right(at, carry):
        for copy in hop(1, at):
            copy.wait_send()
        return carry

    lax.fori_loop(0, jnp.where(chip < last, from_right, 0), drain_left, 0)
    lax.fori_loop(0, jnp.where(chip > 0, from_left, 0), drain_right, 0)

    @pl.when(at_end)
    def _():
        for unit in range(units):
            edge_grad_copy(unit).wait_send()
        for rank in range(last):
            edge_copy(rank, 0).wait_send()
            edge_copy(rank, 1).wait_send()

    @pl.when(next_to_end)
    def _():
        for unit in range(units):
            pass_copy(unit, core).wait_send()

    for unit in range(units):
        sibling_grad(unit).wait_send()
    for target in range(chips):

        @pl.when(needs(target))
        def _(target=target):
            sibling_copy(target).wait_send()

    def drain(unit, carry):
        for copy in gossip(unit):
            copy.wait_send()
        new_copy(unit).wait()
        mixed_copy(unit).wait()
        return carry

    lax.fori_loop(0, units, drain, 0)


def step_with(level, replicas, members, tokens, grads_out, weights, moments):
    chips = members // 2
    last = chips - 1
    held = tokens.shape[0]
    columns = grads_out.shape[1]
    features = weights.shape[1]
    width = min(LANES, columns)
    units = columns // width
    groups = features // GROUP
    passed = (last - 1) * units
    dma = pltpu.SemaphoreType.DMA
    return pl.pallas_call(
        functools.partial(kernel, replicas, chips, 1 << level, float((held * members) ** -0.5)),
        out_shape=(
            jax.ShapeDtypeStruct(weights.shape, jnp.bfloat16),
            jax.ShapeDtypeStruct(moments.shape, jnp.float32),
        ),
        in_specs=[pl.BlockSpec(memory_space=pl.ANY)] * 4,
        out_specs=[pl.BlockSpec(memory_space=pl.ANY)] * 2,
        scratch_shapes=[
            pltpu.VMEM((chips, 2, held, features), jnp.bfloat16),
            pltpu.VMEM((units, 2, held, width), jnp.bfloat16),
            pltpu.VMEM((last, 2, held, features), jnp.bfloat16),
            pltpu.VMEM((units, 2, held, width), jnp.bfloat16),
            pltpu.VMEM((2, passed, features, width), jnp.int16),
            pltpu.VMEM((2, passed, groups, width), jnp.float32),
            pltpu.VMEM((3, features, width), jnp.float32),
            pltpu.VMEM((units, features, width), jnp.bfloat16),
            pltpu.VMEM((units, features, width), jnp.float32),
            pltpu.VMEM((units, features, width), jnp.float32),
            pltpu.VMEM((units, features, width), jnp.float32),
            pltpu.VMEM((units, features, width), jnp.bfloat16),
            pltpu.VMEM((units, features, width), jnp.int16),
            pltpu.VMEM((units, groups, width), jnp.float32),
            pltpu.VMEM((units, features, width), jnp.int16),
            pltpu.VMEM((units, groups, width), jnp.float32),
            dma((chips,)),
            dma((chips,)),
            dma((chips,)),
            dma((units,)),
            dma((units,)),
            dma((units,)),
            dma((2, units)),
            dma((last, 2)),
            dma((last, 2)),
            dma((units,)),
            dma((units,)),
            dma((units,)),
            dma((units,)),
            dma((2, passed)),
            dma((2, passed)),
            dma((2, passed)),
            dma((2, passed)),
            dma((units,)),
            dma((units,)),
            dma((units,)),
            dma((units,)),
            dma((units,)),
            dma((units,)),
        ],
        compiler_params=pltpu.CompilerParams(
            collective_id=level, has_side_effects=True, vmem_limit_bytes=44 * 1024 * 1024
        ),
        cost_estimate=pl.CostEstimate(
            flops=2 * held * members * features * columns,
            bytes_accessed=2 * tokens.size + 10 * features * columns,
            transcendentals=0,
        ),
    )(tokens, grads_out, weights, moments)


def solution(mesh):
    replicas, members = mesh.shape["replica"], mesh.shape["fsdp"]
    levels = replicas.bit_length() - 1

    def body(tokens, grads_out, weights, moments, step):
        level = step[0] % levels
        branches = [
            functools.partial(step_with, power, replicas, members) for power in range(levels)
        ]
        return lax.switch(level, branches, tokens, grads_out, weights, moments)

    return jax.shard_map(
        body,
        mesh=mesh,
        in_specs=(
            P(("replica", "fsdp"), None),
            P(("replica", "fsdp"), None),
            P("replica", "fsdp", None),
            P("replica", "fsdp", None),
            P(),
        ),
        out_specs=(P("replica", "fsdp", None), P("replica", "fsdp", None)),
        check_vma=False,
    )
```

```python
import functools

import jax
import jax.numpy as jnp
from jax import lax
from jax.experimental import pallas as pl
from jax.experimental.pallas import tpu as pltpu
from jax.sharding import PartitionSpec as P

MESH = pl.DeviceIdType.MESH
TOP = 32767.0
TINY = 1e-30
HOP = 2
LANES = 256
GROUP = 256


def kernel(
    replicas,
    chips,
    distance,
    scale,
    tokens_hbm,
    grads_hbm,
    weights_hbm,
    moments_hbm,
    mixed_hbm,
    new_hbm,
    tok,
    grad,
    edge_tok,
    edge_grad,
    buf,
    factor,
    part,
    weights,
    moments,
    new,
    updated,
    mixed,
    out_buf,
    out_factor,
    in_buf,
    in_factor,
    own_sem,
    sib_send,
    sib_recv,
    own_grad_sem,
    sib_grad_send,
    sib_grad_recv,
    load_sem,
    edge_send,
    edge_recv,
    edge_grad_send,
    edge_grad_recv,
    pass_send,
    pass_recv,
    send,
    recv,
    factor_send,
    factor_recv,
    gossip_send,
    gossip_recv,
    gossip_factor_send,
    gossip_factor_recv,
    new_sem,
    mixed_sem,
):
    last = chips - 1
    units, features, width = updated.shape
    replica = lax.axis_index("replica")
    me = lax.axis_index("fsdp")
    chip = me // 2
    core = me % 2
    sibling = chip * 2 + 1 - core
    left = jnp.maximum(me - 2, 0)
    right = jnp.minimum(me + 2, 2 * chips - 1)
    partner = (replica + distance) % replicas
    source = (replica + replicas - distance) % replicas
    at_end = jnp.logical_or(chip == 0, chip == last)
    next_to_end = jnp.logical_or(chip == 1, chip == last - 1)
    high = chip >= chips // 2
    inner = jnp.where(high, last - 1, 1)
    outer = jnp.where(high, last, 0)

    def span(unit):
        return pl.ds(pl.multiple_of(unit * width, width), width)

    def remote(source_ref, to_ref, send_sem, recv_sem, device):
        return pltpu.make_async_remote_copy(
            src_ref=source_ref,
            dst_ref=to_ref,
            send_sem=send_sem,
            recv_sem=recv_sem,
            device_id=device,
            device_id_type=MESH,
        )

    def piece(target, which):
        start = pl.multiple_of((2 * target + which) * features, features)
        return tokens_hbm.at[:, pl.ds(start, features)]

    def own_copy(target):
        return pltpu.make_async_copy(piece(target, core), tok.at[target, core], own_sem.at[target])

    def sibling_copy(target):
        return remote(
            piece(target, 1 - core),
            tok.at[target, core],
            sib_send.at[target],
            sib_recv.at[target],
            {"fsdp": sibling},
        )

    def own_grad(unit):
        return pltpu.make_async_copy(
            grads_hbm.at[:, span(unit)], grad.at[unit, core], own_grad_sem.at[unit]
        )

    def sibling_grad(unit):
        return remote(
            grads_hbm.at[:, span(unit)],
            grad.at[unit, core],
            sib_grad_send.at[unit],
            sib_grad_recv.at[unit],
            {"fsdp": sibling},
        )

    def edge_target(rank):
        return jnp.where(high, rank, last - rank)

    def edge_copy(rank, which):
        return remote(
            piece(edge_target(rank), which),
            edge_tok.at[rank, core],
            edge_send.at[rank, which],
            edge_recv.at[rank, core],
            {"fsdp": inner * 2 + which},
        )

    def edge_arrival(rank, which):
        return remote(
            edge_tok.at[rank, which],
            edge_tok.at[rank, which],
            edge_send.at[rank, which],
            edge_recv.at[rank, which],
            {"fsdp": sibling},
        )

    def edge_grad_copy(unit):
        return remote(
            grads_hbm.at[:, span(unit)],
            edge_grad.at[unit, core],
            edge_grad_send.at[unit],
            edge_grad_recv.at[unit],
            {"fsdp": inner * 2 + core},
        )

    def edge_grad_arrival(unit):
        return remote(
            edge_grad.at[unit, core],
            edge_grad.at[unit, core],
            edge_grad_send.at[unit],
            edge_grad_recv.at[unit],
            {"fsdp": sibling},
        )

    def pass_copy(unit, which):
        return remote(
            edge_grad.at[unit, which],
            edge_grad.at[unit, which],
            pass_send.at[unit],
            pass_recv.at[unit],
            {"fsdp": sibling},
        )

    def load(unit):
        return (
            pltpu.make_async_copy(
                weights_hbm.at[0, :, span(unit)], weights.at[unit], load_sem.at[0, unit]
            ),
            pltpu.make_async_copy(
                moments_hbm.at[0, :, span(unit)], moments.at[unit], load_sem.at[1, unit]
            ),
        )

    def hop(way, slot):
        device = {"fsdp": left if way == 0 else right}
        return (
            remote(
                buf.at[way, slot],
                buf.at[way, slot],
                send.at[way, slot],
                recv.at[way, slot],
                device,
            ),
            remote(
                factor.at[way, slot],
                factor.at[way, slot],
                factor_send.at[way, slot],
                factor_recv.at[way, slot],
                device,
            ),
        )

    def gossip(unit):
        device = {"replica": partner}
        return (
            remote(
                out_buf.at[unit],
                in_buf.at[unit],
                gossip_send.at[unit],
                gossip_recv.at[unit],
                device,
            ),
            remote(
                out_factor.at[unit],
                in_factor.at[unit],
                gossip_factor_send.at[unit],
                gossip_factor_recv.at[unit],
                device,
            ),
        )

    def new_copy(unit):
        return pltpu.make_async_copy(new.at[unit], new_hbm.at[0, :, span(unit)], new_sem.at[unit])

    def mixed_copy(unit):
        return pltpu.make_async_copy(
            mixed.at[unit], mixed_hbm.at[0, :, span(unit)], mixed_sem.at[unit]
        )

    order = []
    for near in range(chips // 2):
        order += [near, last - near]

    barrier = pltpu.get_barrier_semaphore()
    pl.semaphore_signal(barrier, inc=1, device_id={"fsdp": sibling}, device_id_type=MESH)
    pl.semaphore_signal(barrier, inc=1, device_id={"replica": source}, device_id_type=MESH)

    @pl.when(chip > 0)
    def _():
        pl.semaphore_signal(barrier, inc=1, device_id={"fsdp": left}, device_id_type=MESH)

    @pl.when(chip < last)
    def _():
        pl.semaphore_signal(barrier, inc=1, device_id={"fsdp": right}, device_id_type=MESH)

    @pl.when(next_to_end)
    def _():
        pl.semaphore_signal(
            barrier, inc=1, device_id={"fsdp": outer * 2 + 1 - core}, device_id_type=MESH
        )

    for unit in range(units):
        own_grad(unit).start()
    def needs(target):
        return jnp.logical_or(jnp.logical_not(at_end), chip == target)

    for target in order:

        @pl.when(needs(target))
        def _(target=target):
            own_copy(target).start()

    pl.semaphore_wait(barrier, 4)

    @pl.when(at_end)
    def _():
        edge_grad_copy(0).start()
        edge_copy(0, 0).start()
        edge_copy(0, 1).start()

    for unit in range(units):
        sibling_grad(unit).start()
    for target in order:

        @pl.when(needs(target))
        def _(target=target):
            sibling_copy(target).start()

    @pl.when(at_end)
    def _():
        for unit in range(1, units):
            edge_grad_copy(unit).start()
        for rank in range(1, last):
            edge_copy(rank, 0).start()
            edge_copy(rank, 1).start()

    for unit in range(units):
        for copy in load(unit):
            copy.start()

    for unit in range(units):
        own_grad(unit).wait()
        sibling_grad(unit).wait_recv()

    def dot(a, b):
        return lax.dot_general(
            a.reshape(-1, a.shape[-1]),
            b.reshape(-1, b.shape[-1]),
            (((0,), (0,)), ((), ())),
            preferred_element_type=jnp.float32,
        )

    def decode(data, factors):
        return data.astype(jnp.int32).astype(jnp.float32) * factors

    def encode(value):
        largest = jnp.max(jnp.abs(value), axis=0, keepdims=True)
        largest = jnp.maximum(largest, TINY)
        code = jnp.round(value * (TOP / largest * (1.0 - 1e-6)))
        return code.astype(jnp.int32).astype(jnp.int16), largest * (1.0 / TOP / (1.0 - 1e-6))

    groups = [(g, slice(g * GROUP, (g + 1) * GROUP)) for g in range(features // GROUP)]

    def multiply(slot, target, rank, unit, with_edge):
        @pl.when(unit == 0)
        def _():
            own_copy(target).wait()
            sibling_copy(target).wait_recv()

        part[slot] = dot(tok[target], grad[unit])

        @pl.when(with_edge)
        def _():
            @pl.when(rank == 0)
            def _():
                edge_grad_arrival(unit).wait_recv()
                pass_copy(unit, core).start()
                pass_copy(unit, 1 - core).wait_recv()

            @pl.when(unit == 0)
            def _():
                edge_arrival(rank, 0).wait_recv()
                edge_arrival(rank, 1).wait_recv()

            part[slot] += dot(edge_tok[rank], edge_grad[unit])

    def receive(slot, way, at):
        for copy in hop(way, at):
            copy.wait_recv()
        for g, rows in groups:
            part[slot, rows] += decode(buf[way, at, rows], factor[way, at, g : g + 1])

    def forward(way, at, beside_end):
        rank = at // units
        multiply(way, rank if way == 0 else last - rank, rank, at % units, beside_end)

        @pl.when(jnp.logical_not(beside_end))
        def _():
            receive(way, way, at)

        for g, rows in groups:
            buf[way, at, rows], factor[way, at, g : g + 1] = encode(part[way, rows])
        for copy in hop(way, at):
            copy.start()

    from_right = chip * units
    from_left = (last - chip) * units
    lag_right = jnp.maximum(last - 1 - chip, 0) * HOP
    lag_left = jnp.maximum(chip - 1, 0) * HOP
    largest_slot = (last - 1) * units - 1

    def finish(unit):
        multiply(2, chip, last - 1, unit, next_to_end)

        @pl.when(chip < last - 1)
        def _():
            receive(2, 0, jnp.minimum(from_right + unit, largest_slot))

        @pl.when(chip > 1)
        def _():
            receive(2, 1, jnp.minimum(from_left + unit, largest_slot))

        for copy in load(unit):
            copy.wait()
        for g, rows in groups:
            moment = 0.9 * moments[unit, rows] + part[2, rows] * scale
            new[unit, rows] = moment
            value = weights[unit, rows].astype(jnp.float32) - 0.05 * moment
            updated[unit, rows] = value
            out_buf[unit, rows], out_factor[unit, g : g + 1] = encode(value)
        for copy in gossip(unit):
            copy.start()
        new_copy(unit).start()

    begin_finish = jnp.maximum(
        jnp.where(chip < last, from_right + lag_right, 0),
        jnp.where(chip > 0, from_left + lag_left, 0),
    )

    def step(i, carry):
        at_l = i - lag_right
        at_r = i - lag_left
        unit = i - begin_finish

        @pl.when((at_l >= 0) & (at_l < from_right) & (chip < last))
        def _():
            forward(0, at_l, chip == last - 1)

        @pl.when((at_r >= 0) & (at_r < from_left) & (chip > 0))
        def _():
            forward(1, at_r, chip == 1)

        @pl.when((unit >= 0) & (unit < units))
        def _():
            finish(unit)

        return carry

    steps = (last - 1) * max(units, HOP) + units + HOP
    lax.fori_loop(0, steps, step, 0)

    def mix(unit, carry):
        for copy in gossip(unit):
            copy.wait_recv()
        for g, rows in groups:
            theirs = decode(in_buf[unit, rows], in_factor[unit, g : g + 1])
            mixed[unit, rows] = ((updated[unit, rows] + theirs) * 0.5).astype(jnp.bfloat16)
        mixed_copy(unit).start()
        return carry

    lax.fori_loop(0, units, mix, 0)

    def drain_left(at, carry):
        for copy in hop(0, at):
            copy.wait_send()
        return carry

    def drain_right(at, carry):
        for copy in hop(1, at):
            copy.wait_send()
        return carry

    lax.fori_loop(0, jnp.where(chip < last, from_right, 0), drain_left, 0)
    lax.fori_loop(0, jnp.where(chip > 0, from_left, 0), drain_right, 0)

    @pl.when(at_end)
    def _():
        for unit in range(units):
            edge_grad_copy(unit).wait_send()
        for rank in range(last):
            edge_copy(rank, 0).wait_send()
            edge_copy(rank, 1).wait_send()

    @pl.when(next_to_end)
    def _():
        for unit in range(units):
            pass_copy(unit, core).wait_send()

    for unit in range(units):
        sibling_grad(unit).wait_send()
    for target in range(chips):

        @pl.when(needs(target))
        def _(target=target):
            sibling_copy(target).wait_send()

    def drain(unit, carry):
        for copy in gossip(unit):
            copy.wait_send()
        new_copy(unit).wait()
        mixed_copy(unit).wait()
        return carry

    lax.fori_loop(0, units, drain, 0)


def step_with(level, replicas, members, tokens, grads_out, weights, moments):
    chips = members // 2
    last = chips - 1
    held = tokens.shape[0]
    columns = grads_out.shape[1]
    features = weights.shape[1]
    width = min(LANES, columns)
    units = columns // width
    groups = features // GROUP
    passed = (last - 1) * units
    dma = pltpu.SemaphoreType.DMA
    return pl.pallas_call(
        functools.partial(kernel, replicas, chips, 1 << level, float((held * members) ** -0.5)),
        out_shape=(
            jax.ShapeDtypeStruct(weights.shape, jnp.bfloat16),
            jax.ShapeDtypeStruct(moments.shape, jnp.float32),
        ),
        in_specs=[pl.BlockSpec(memory_space=pl.ANY)] * 4,
        out_specs=[pl.BlockSpec(memory_space=pl.ANY)] * 2,
        scratch_shapes=[
            pltpu.VMEM((chips, 2, held, features), jnp.bfloat16),
            pltpu.VMEM((units, 2, held, width), jnp.bfloat16),
            pltpu.VMEM((last, 2, held, features), jnp.bfloat16),
            pltpu.VMEM((units, 2, held, width), jnp.bfloat16),
            pltpu.VMEM((2, passed, features, width), jnp.int16),
            pltpu.VMEM((2, passed, groups, width), jnp.float32),
            pltpu.VMEM((3, features, width), jnp.float32),
            pltpu.VMEM((units, features, width), jnp.bfloat16),
            pltpu.VMEM((units, features, width), jnp.float32),
            pltpu.VMEM((units, features, width), jnp.float32),
            pltpu.VMEM((units, features, width), jnp.float32),
            pltpu.VMEM((units, features, width), jnp.bfloat16),
            pltpu.VMEM((units, features, width), jnp.int16),
            pltpu.VMEM((units, groups, width), jnp.float32),
            pltpu.VMEM((units, features, width), jnp.int16),
            pltpu.VMEM((units, groups, width), jnp.float32),
            dma((chips,)),
            dma((chips,)),
            dma((chips,)),
            dma((units,)),
            dma((units,)),
            dma((units,)),
            dma((2, units)),
            dma((last, 2)),
            dma((last, 2)),
            dma((units,)),
            dma((units,)),
            dma((units,)),
            dma((units,)),
            dma((2, passed)),
            dma((2, passed)),
            dma((2, passed)),
            dma((2, passed)),
            dma((units,)),
            dma((units,)),
            dma((units,)),
            dma((units,)),
            dma((units,)),
            dma((units,)),
        ],
        compiler_params=pltpu.CompilerParams(
            collective_id=level, has_side_effects=True, vmem_limit_bytes=44 * 1024 * 1024
        ),
        cost_estimate=pl.CostEstimate(
            flops=2 * held * members * features * columns,
            bytes_accessed=2 * tokens.size + 10 * features * columns,
            transcendentals=0,
        ),
    )(tokens, grads_out, weights, moments)


def solution(mesh):
    replicas, members = mesh.shape["replica"], mesh.shape["fsdp"]
    levels = replicas.bit_length() - 1

    def body(tokens, grads_out, weights, moments, step):
        level = step[0] % levels
        branches = [
            functools.partial(step_with, power, replicas, members) for power in range(levels)
        ]
        return lax.switch(level, branches, tokens, grads_out, weights, moments)

    return jax.shard_map(
        body,
        mesh=mesh,
        in_specs=(
            P(("replica", "fsdp"), None),
            P(("replica", "fsdp"), None),
            P("replica", "fsdp", None),
            P("replica", "fsdp", None),
            P(),
        ),
        out_specs=(P("replica", "fsdp", None), P("replica", "fsdp", None)),
        check_vma=False,
    )
```

```python
import functools

import jax
import jax.numpy as jnp
from jax import lax
from jax.experimental import pallas as pl
from jax.experimental.pallas import tpu as pltpu
from jax.sharding import PartitionSpec as P

MESH = pl.DeviceIdType.MESH
TOP = 32767.0
TINY = 1e-30
HOP = 2
LANES = 256


def kernel(
    replicas,
    chips,
    distance,
    scale,
    tokens_hbm,
    grads_hbm,
    weights_hbm,
    moments_hbm,
    mixed_hbm,
    new_hbm,
    tok,
    grad,
    edge_tok,
    edge_grad,
    buf,
    factor,
    part,
    weights,
    moments,
    new,
    updated,
    mixed,
    out_buf,
    out_factor,
    in_buf,
    in_factor,
    own_sem,
    sib_send,
    sib_recv,
    own_grad_sem,
    sib_grad_send,
    sib_grad_recv,
    load_sem,
    edge_send,
    edge_recv,
    edge_grad_send,
    edge_grad_recv,
    pass_send,
    pass_recv,
    send,
    recv,
    factor_send,
    factor_recv,
    half_send,
    half_recv,
    gossip_send,
    gossip_recv,
    gossip_factor_send,
    gossip_factor_recv,
    new_sem,
    mixed_sem,
):
    last = chips - 1
    units, features, width = updated.shape
    replica = lax.axis_index("replica")
    me = lax.axis_index("fsdp")
    chip = me // 2
    core = me % 2
    sibling = chip * 2 + 1 - core
    left = jnp.maximum(me - 2, 0)
    right = jnp.minimum(me + 2, 2 * chips - 1)
    partner = (replica + distance) % replicas
    source = (replica + replicas - distance) % replicas
    at_end = jnp.logical_or(chip == 0, chip == last)
    next_to_end = jnp.logical_or(chip == 1, chip == last - 1)
    high = chip >= chips // 2
    inner = jnp.where(high, last - 1, 1)
    outer = jnp.where(high, last, 0)

    def span(unit):
        return pl.ds(pl.multiple_of(unit * width, width), width)

    def remote(source_ref, to_ref, send_sem, recv_sem, device):
        return pltpu.make_async_remote_copy(
            src_ref=source_ref,
            dst_ref=to_ref,
            send_sem=send_sem,
            recv_sem=recv_sem,
            device_id=device,
            device_id_type=MESH,
        )

    def piece(target, which):
        start = pl.multiple_of((2 * target + which) * features, features)
        return tokens_hbm.at[:, pl.ds(start, features)]

    def own_copy(target):
        return pltpu.make_async_copy(piece(target, core), tok.at[target, core], own_sem.at[target])

    def sibling_copy(target):
        return remote(
            piece(target, 1 - core),
            tok.at[target, core],
            sib_send.at[target],
            sib_recv.at[target],
            {"fsdp": sibling},
        )

    def own_grad(unit):
        return pltpu.make_async_copy(
            grads_hbm.at[:, span(unit)], grad.at[unit, core], own_grad_sem.at[unit]
        )

    def sibling_grad(unit):
        return remote(
            grads_hbm.at[:, span(unit)],
            grad.at[unit, core],
            sib_grad_send.at[unit],
            sib_grad_recv.at[unit],
            {"fsdp": sibling},
        )

    def edge_target(rank):
        return jnp.where(high, rank, last - rank)

    def edge_copy(rank, which):
        return remote(
            piece(edge_target(rank), which),
            edge_tok.at[rank, core],
            edge_send.at[rank, which],
            edge_recv.at[rank, core],
            {"fsdp": inner * 2 + which},
        )

    def edge_arrival(rank, which):
        return remote(
            edge_tok.at[rank, which],
            edge_tok.at[rank, which],
            edge_send.at[rank, which],
            edge_recv.at[rank, which],
            {"fsdp": sibling},
        )

    def edge_grad_copy(unit):
        return remote(
            grads_hbm.at[:, span(unit)],
            edge_grad.at[unit, core],
            edge_grad_send.at[unit],
            edge_grad_recv.at[unit],
            {"fsdp": inner * 2 + core},
        )

    def edge_grad_arrival(unit):
        return remote(
            edge_grad.at[unit, core],
            edge_grad.at[unit, core],
            edge_grad_send.at[unit],
            edge_grad_recv.at[unit],
            {"fsdp": sibling},
        )

    def pass_copy(unit, which):
        return remote(
            edge_grad.at[unit, which],
            edge_grad.at[unit, which],
            pass_send.at[unit],
            pass_recv.at[unit],
            {"fsdp": sibling},
        )

    def load(unit):
        return (
            pltpu.make_async_copy(
                weights_hbm.at[0, :, span(unit)], weights.at[unit], load_sem.at[0, unit]
            ),
            pltpu.make_async_copy(
                moments_hbm.at[0, :, span(unit)], moments.at[unit], load_sem.at[1, unit]
            ),
        )

    half = features // 2

    def half_rows(part_of):
        return pl.ds(pl.multiple_of(part_of * half, half), half)

    def hop_whole(way, slot):
        return remote(
            buf.at[way, slot],
            buf.at[way, slot],
            send.at[way, slot],
            recv.at[way, slot],
            {"fsdp": left if way == 0 else right},
        )

    def hop_half(way, slot, part_of):
        at = buf.at[way, slot, half_rows(part_of)]
        if part_of == 0:
            sems = send.at[way, slot], recv.at[way, slot]
        else:
            sems = half_send.at[way, slot % units], half_recv.at[way, slot % units]
        return remote(at, at, *sems, {"fsdp": left if way == 0 else right})

    def hop_factor(way, slot):
        return remote(
            factor.at[way, slot],
            factor.at[way, slot],
            factor_send.at[way, slot],
            factor_recv.at[way, slot],
            {"fsdp": left if way == 0 else right},
        )

    def is_late(slot):
        return slot // units == last - 2

    def gossip(unit, part_of):
        device = {"replica": partner}
        rows = half_rows(part_of)
        return (
            remote(
                out_buf.at[unit, rows],
                in_buf.at[unit, rows],
                gossip_send.at[unit, part_of],
                gossip_recv.at[unit, part_of],
                device,
            ),
            remote(
                out_factor.at[unit, part_of],
                in_factor.at[unit, part_of],
                gossip_factor_send.at[unit, part_of],
                gossip_factor_recv.at[unit, part_of],
                device,
            ),
        )

    def new_copy(unit):
        return pltpu.make_async_copy(new.at[unit], new_hbm.at[0, :, span(unit)], new_sem.at[unit])

    def mixed_copy(unit, part_of):
        rows = half_rows(part_of)
        return pltpu.make_async_copy(
            mixed.at[unit, rows],
            mixed_hbm.at[0, rows, span(unit)],
            mixed_sem.at[unit, part_of],
        )

    order = []
    for near in range(chips // 2):
        order += [near, last - near]

    barrier = pltpu.get_barrier_semaphore()
    pl.semaphore_signal(barrier, inc=1, device_id={"fsdp": sibling}, device_id_type=MESH)
    pl.semaphore_signal(barrier, inc=1, device_id={"replica": source}, device_id_type=MESH)

    @pl.when(chip > 0)
    def _():
        pl.semaphore_signal(barrier, inc=1, device_id={"fsdp": left}, device_id_type=MESH)

    @pl.when(chip < last)
    def _():
        pl.semaphore_signal(barrier, inc=1, device_id={"fsdp": right}, device_id_type=MESH)

    @pl.when(next_to_end)
    def _():
        pl.semaphore_signal(
            barrier, inc=1, device_id={"fsdp": outer * 2 + 1 - core}, device_id_type=MESH
        )

    for unit in range(units):
        own_grad(unit).start()
    def needs(target):
        return jnp.logical_or(jnp.logical_not(at_end), chip == target)

    for target in order:

        @pl.when(needs(target))
        def _(target=target):
            own_copy(target).start()

    pl.semaphore_wait(barrier, 4)

    @pl.when(at_end)
    def _():
        edge_grad_copy(0).start()
        edge_copy(0, 0).start()
        edge_copy(0, 1).start()

    for unit in range(units):
        sibling_grad(unit).start()
    for target in order:

        @pl.when(needs(target))
        def _(target=target):
            sibling_copy(target).start()

    @pl.when(at_end)
    def _():
        for unit in range(1, units):
            edge_grad_copy(unit).start()
        for rank in range(1, last):
            edge_copy(rank, 0).start()
            edge_copy(rank, 1).start()

    for unit in range(units):
        for copy in load(unit):
            copy.start()

    for unit in range(units):
        own_grad(unit).wait()
        sibling_grad(unit).wait_recv()

    def dot(a, b):
        return lax.dot_general(
            a.reshape(-1, a.shape[-1]),
            b.reshape(-1, b.shape[-1]),
            (((0,), (0,)), ((), ())),
            preferred_element_type=jnp.float32,
        )

    def decode(data, factors):
        return data.astype(jnp.int32).astype(jnp.float32) * factors

    def encode(value):
        largest = jnp.max(jnp.abs(value), axis=0, keepdims=True)
        largest = jnp.maximum(largest, TINY)
        code = jnp.round(value * (TOP / largest * (1.0 - 1e-6)))
        return code.astype(jnp.int32).astype(jnp.int16), largest * (1.0 / TOP / (1.0 - 1e-6))

    def multiply(slot, target, rank, unit, with_edge):
        @pl.when(unit == 0)
        def _():
            own_copy(target).wait()
            sibling_copy(target).wait_recv()

        part[slot] = dot(tok[target], grad[unit])

        @pl.when(with_edge)
        def _():
            @pl.when(rank == 0)
            def _():
                edge_grad_arrival(unit).wait_recv()
                pass_copy(unit, core).start()
                pass_copy(unit, 1 - core).wait_recv()

            @pl.when(unit == 0)
            def _():
                edge_arrival(rank, 0).wait_recv()
                edge_arrival(rank, 1).wait_recv()

            part[slot] += dot(edge_tok[rank], edge_grad[unit])

    def forward(way, at, beside_end):
        rank = at // units
        multiply(way, rank if way == 0 else last - rank, rank, at % units, beside_end)

        @pl.when(jnp.logical_not(beside_end))
        def _():
            hop_factor(way, at).wait_recv()
            hop_whole(way, at).wait_recv()
            part[way] += decode(buf[way, at], factor[way, at])

        buf[way, at], factor[way, at] = encode(part[way])
        hop_factor(way, at).start()

        @pl.when(is_late(at))
        def _():
            hop_half(way, at, 0).start()
            hop_half(way, at, 1).start()

        @pl.when(jnp.logical_not(is_late(at)))
        def _():
            hop_whole(way, at).start()

    from_right = chip * units
    from_left = (last - chip) * units
    lag_right = jnp.maximum(last - 1 - chip, 0) * HOP
    lag_left = jnp.maximum(chip - 1, 0) * HOP
    largest_slot = (last - 1) * units - 1

    def finish(unit):
        multiply(2, chip, last - 1, unit, next_to_end)

        for part_of in range(2):
            rows = slice(part_of * half, (part_of + 1) * half)

            for way, begin, there in ((0, from_right, chip < last - 1), (1, from_left, chip > 1)):

                @pl.when(there)
                def _(way=way, begin=begin):
                    at = jnp.minimum(begin + unit, largest_slot)
                    late = is_late(at)
                    if part_of == 0:
                        hop_factor(way, at).wait_recv()

                        @pl.when(jnp.logical_not(late))
                        def _():
                            hop_whole(way, at).wait_recv()

                    @pl.when(late)
                    def _():
                        hop_half(way, at, part_of).wait_recv()

                    part[2, rows] += decode(buf[way, at, rows], factor[way, at])

            if part_of == 0:
                for copy in load(unit):
                    copy.wait()
            moment = 0.9 * moments[unit, rows] + part[2, rows] * scale
            new[unit, rows] = moment
            value = weights[unit, rows].astype(jnp.float32) - 0.05 * moment
            updated[unit, rows] = value
            out_buf[unit, rows], out_factor[unit, part_of] = encode(value)
            for copy in gossip(unit, part_of):
                copy.start()
        new_copy(unit).start()

    begin_finish = jnp.maximum(
        jnp.where(chip < last, from_right + lag_right, 0),
        jnp.where(chip > 0, from_left + lag_left, 0),
    )

    def step(i, carry):
        at_l = i - lag_right
        at_r = i - lag_left
        unit = i - begin_finish

        @pl.when((at_l >= 0) & (at_l < from_right) & (chip < last))
        def _():
            forward(0, at_l, chip == last - 1)

        @pl.when((at_r >= 0) & (at_r < from_left) & (chip > 0))
        def _():
            forward(1, at_r, chip == 1)

        @pl.when((unit >= 0) & (unit < units))
        def _():
            finish(unit)

        return carry

    steps = (last - 1) * max(units, HOP) + units + HOP
    lax.fori_loop(0, steps, step, 0)

    def mix(i, carry):
        unit, part_of = i // 2, i % 2
        for copy in gossip(unit, part_of):
            copy.wait_recv()
        rows = half_rows(part_of)
        theirs = decode(in_buf[unit, rows], in_factor[unit, part_of])
        mixed[unit, rows] = ((updated[unit, rows] + theirs) * 0.5).astype(jnp.bfloat16)
        mixed_copy(unit, part_of).start()
        return carry

    lax.fori_loop(0, 2 * units, mix, 0)

    def drain_way(way, at):
        hop_factor(way, at).wait_send()

        @pl.when(is_late(at))
        def _():
            hop_half(way, at, 0).wait_send()
            hop_half(way, at, 1).wait_send()

        @pl.when(jnp.logical_not(is_late(at)))
        def _():
            hop_whole(way, at).wait_send()

    def drain_left(at, carry):
        drain_way(0, at)
        return carry

    def drain_right(at, carry):
        drain_way(1, at)
        return carry

    lax.fori_loop(0, jnp.where(chip < last, from_right, 0), drain_left, 0)
    lax.fori_loop(0, jnp.where(chip > 0, from_left, 0), drain_right, 0)

    @pl.when(at_end)
    def _():
        for unit in range(units):
            edge_grad_copy(unit).wait_send()
        for rank in range(last):
            edge_copy(rank, 0).wait_send()
            edge_copy(rank, 1).wait_send()

    @pl.when(next_to_end)
    def _():
        for unit in range(units):
            pass_copy(unit, core).wait_send()

    for unit in range(units):
        sibling_grad(unit).wait_send()
    for target in range(chips):

        @pl.when(needs(target))
        def _(target=target):
            sibling_copy(target).wait_send()

    def drain(unit, carry):
        new_copy(unit).wait()
        for part_of in range(2):
            for copy in gossip(unit, part_of):
                copy.wait_send()
            mixed_copy(unit, part_of).wait()
        return carry

    lax.fori_loop(0, units, drain, 0)


def step_with(level, replicas, members, tokens, grads_out, weights, moments):
    chips = members // 2
    last = chips - 1
    held = tokens.shape[0]
    columns = grads_out.shape[1]
    features = weights.shape[1]
    width = min(LANES, columns)
    units = columns // width
    passed = (last - 1) * units
    dma = pltpu.SemaphoreType.DMA
    return pl.pallas_call(
        functools.partial(kernel, replicas, chips, 1 << level, float((held * members) ** -0.5)),
        out_shape=(
            jax.ShapeDtypeStruct(weights.shape, jnp.bfloat16),
            jax.ShapeDtypeStruct(moments.shape, jnp.float32),
        ),
        in_specs=[pl.BlockSpec(memory_space=pl.ANY)] * 4,
        out_specs=[pl.BlockSpec(memory_space=pl.ANY)] * 2,
        scratch_shapes=[
            pltpu.VMEM((chips, 2, held, features), jnp.bfloat16),
            pltpu.VMEM((units, 2, held, width), jnp.bfloat16),
            pltpu.VMEM((last, 2, held, features), jnp.bfloat16),
            pltpu.VMEM((units, 2, held, width), jnp.bfloat16),
            pltpu.VMEM((2, passed, features, width), jnp.int16),
            pltpu.VMEM((2, passed, 1, width), jnp.float32),
            pltpu.VMEM((3, features, width), jnp.float32),
            pltpu.VMEM((units, features, width), jnp.bfloat16),
            pltpu.VMEM((units, features, width), jnp.float32),
            pltpu.VMEM((units, features, width), jnp.float32),
            pltpu.VMEM((units, features, width), jnp.float32),
            pltpu.VMEM((units, features, width), jnp.bfloat16),
            pltpu.VMEM((units, features, width), jnp.int16),
            pltpu.VMEM((units, 2, 1, width), jnp.float32),
            pltpu.VMEM((units, features, width), jnp.int16),
            pltpu.VMEM((units, 2, 1, width), jnp.float32),
            dma((chips,)),
            dma((chips,)),
            dma((chips,)),
            dma((units,)),
            dma((units,)),
            dma((units,)),
            dma((2, units)),
            dma((last, 2)),
            dma((last, 2)),
            dma((units,)),
            dma((units,)),
            dma((units,)),
            dma((units,)),
            dma((2, passed)),
            dma((2, passed)),
            dma((2, passed)),
            dma((2, passed)),
            dma((2, units)),
            dma((2, units)),
            dma((units, 2)),
            dma((units, 2)),
            dma((units, 2)),
            dma((units, 2)),
            dma((units,)),
            dma((units, 2)),
        ],
        compiler_params=pltpu.CompilerParams(
            collective_id=level, has_side_effects=True, vmem_limit_bytes=44 * 1024 * 1024
        ),
        cost_estimate=pl.CostEstimate(
            flops=2 * held * members * features * columns,
            bytes_accessed=2 * tokens.size + 10 * features * columns,
            transcendentals=0,
        ),
    )(tokens, grads_out, weights, moments)


def solution(mesh):
    replicas, members = mesh.shape["replica"], mesh.shape["fsdp"]
    levels = replicas.bit_length() - 1

    def body(tokens, grads_out, weights, moments, step):
        level = step[0] % levels
        branches = [
            functools.partial(step_with, power, replicas, members) for power in range(levels)
        ]
        return lax.switch(level, branches, tokens, grads_out, weights, moments)

    return jax.shard_map(
        body,
        mesh=mesh,
        in_specs=(
            P(("replica", "fsdp"), None),
            P(("replica", "fsdp"), None),
            P("replica", "fsdp", None),
            P("replica", "fsdp", None),
            P(),
        ),
        out_specs=(P("replica", "fsdp", None), P("replica", "fsdp", None)),
        check_vma=False,
    )
```

```python
import functools

import jax
import jax.numpy as jnp
from jax import lax
from jax.experimental import pallas as pl
from jax.experimental.pallas import tpu as pltpu
from jax.sharding import PartitionSpec as P

MESH = pl.DeviceIdType.MESH
TOP = 32767.0
TINY = 1e-30
HOP = 3
LANES = 256


def kernel(
    replicas,
    chips,
    distance,
    scale,
    tokens_hbm,
    grads_hbm,
    weights_hbm,
    moments_hbm,
    mixed_hbm,
    new_hbm,
    tok,
    grad,
    edge_tok,
    edge_grad,
    buf,
    factor,
    part,
    weights,
    moments,
    new,
    updated,
    mixed,
    out_buf,
    out_factor,
    in_buf,
    in_factor,
    own_sem,
    sib_send,
    sib_recv,
    own_grad_sem,
    sib_grad_send,
    sib_grad_recv,
    load_sem,
    edge_send,
    edge_recv,
    edge_grad_send,
    edge_grad_recv,
    pass_send,
    pass_recv,
    send,
    recv,
    factor_send,
    factor_recv,
    half_send,
    half_recv,
    gossip_send,
    gossip_recv,
    gossip_factor_send,
    gossip_factor_recv,
    new_sem,
    mixed_sem,
):
    last = chips - 1
    units, features, width = updated.shape
    replica = lax.axis_index("replica")
    me = lax.axis_index("fsdp")
    chip = me // 2
    core = me % 2
    sibling = chip * 2 + 1 - core
    left = jnp.maximum(me - 2, 0)
    right = jnp.minimum(me + 2, 2 * chips - 1)
    partner = (replica + distance) % replicas
    source = (replica + replicas - distance) % replicas
    at_end = jnp.logical_or(chip == 0, chip == last)
    next_to_end = jnp.logical_or(chip == 1, chip == last - 1)
    high = chip >= chips // 2
    inner = jnp.where(high, last - 1, 1)
    outer = jnp.where(high, last, 0)

    def span(unit):
        return pl.ds(pl.multiple_of(unit * width, width), width)

    def remote(source_ref, to_ref, send_sem, recv_sem, device):
        return pltpu.make_async_remote_copy(
            src_ref=source_ref,
            dst_ref=to_ref,
            send_sem=send_sem,
            recv_sem=recv_sem,
            device_id=device,
            device_id_type=MESH,
        )

    def piece(target, which):
        start = pl.multiple_of((2 * target + which) * features, features)
        return tokens_hbm.at[:, pl.ds(start, features)]

    def own_copy(target):
        return pltpu.make_async_copy(piece(target, core), tok.at[target, core], own_sem.at[target])

    def sibling_copy(target):
        return remote(
            piece(target, 1 - core),
            tok.at[target, core],
            sib_send.at[target],
            sib_recv.at[target],
            {"fsdp": sibling},
        )

    def own_grad(unit):
        return pltpu.make_async_copy(
            grads_hbm.at[:, span(unit)], grad.at[unit, core], own_grad_sem.at[unit]
        )

    def sibling_grad(unit):
        return remote(
            grads_hbm.at[:, span(unit)],
            grad.at[unit, core],
            sib_grad_send.at[unit],
            sib_grad_recv.at[unit],
            {"fsdp": sibling},
        )

    def edge_target(rank):
        return jnp.where(high, rank, last - rank)

    def edge_copy(rank, which):
        return remote(
            piece(edge_target(rank), which),
            edge_tok.at[rank, core],
            edge_send.at[rank, which],
            edge_recv.at[rank, core],
            {"fsdp": inner * 2 + which},
        )

    def edge_arrival(rank, which):
        return remote(
            edge_tok.at[rank, which],
            edge_tok.at[rank, which],
            edge_send.at[rank, which],
            edge_recv.at[rank, which],
            {"fsdp": sibling},
        )

    def edge_grad_copy(unit):
        return remote(
            grad.at[unit, core],
            edge_grad.at[unit, core],
            edge_grad_send.at[unit],
            edge_grad_recv.at[unit],
            {"fsdp": inner * 2 + core},
        )

    def edge_grad_arrival(unit):
        return remote(
            edge_grad.at[unit, core],
            edge_grad.at[unit, core],
            edge_grad_send.at[unit],
            edge_grad_recv.at[unit],
            {"fsdp": sibling},
        )

    def pass_copy(unit, which):
        return remote(
            edge_grad.at[unit, which],
            edge_grad.at[unit, which],
            pass_send.at[unit],
            pass_recv.at[unit],
            {"fsdp": sibling},
        )

    def load(unit):
        return (
            pltpu.make_async_copy(
                weights_hbm.at[0, :, span(unit)], weights.at[unit], load_sem.at[0, unit]
            ),
            pltpu.make_async_copy(
                moments_hbm.at[0, :, span(unit)], moments.at[unit], load_sem.at[1, unit]
            ),
        )

    half = features // 2

    def half_rows(part_of):
        return pl.ds(pl.multiple_of(part_of * half, half), half)

    def hop_whole(way, slot):
        return remote(
            buf.at[way, slot],
            buf.at[way, slot],
            send.at[way, slot],
            recv.at[way, slot],
            {"fsdp": left if way == 0 else right},
        )

    def hop_half(way, slot, part_of):
        at = buf.at[way, slot, half_rows(part_of)]
        if part_of == 0:
            sems = send.at[way, slot], recv.at[way, slot]
        else:
            sems = half_send.at[way, slot % units], half_recv.at[way, slot % units]
        return remote(at, at, *sems, {"fsdp": left if way == 0 else right})

    def hop_factor(way, slot):
        return remote(
            factor.at[way, slot],
            factor.at[way, slot],
            factor_send.at[way, slot],
            factor_recv.at[way, slot],
            {"fsdp": left if way == 0 else right},
        )

    def is_late(slot):
        return slot // units == last - 2

    def gossip(unit, part_of):
        device = {"replica": partner}
        rows = half_rows(part_of)
        return (
            remote(
                out_buf.at[unit, rows],
                in_buf.at[unit, rows],
                gossip_send.at[unit, part_of],
                gossip_recv.at[unit, part_of],
                device,
            ),
            remote(
                out_factor.at[unit, part_of],
                in_factor.at[unit, part_of],
                gossip_factor_send.at[unit, part_of],
                gossip_factor_recv.at[unit, part_of],
                device,
            ),
        )

    def new_copy(unit):
        return pltpu.make_async_copy(new.at[unit], new_hbm.at[0, :, span(unit)], new_sem.at[unit])

    def mixed_copy(unit, part_of):
        rows = half_rows(part_of)
        return pltpu.make_async_copy(
            mixed.at[unit, rows],
            mixed_hbm.at[0, rows, span(unit)],
            mixed_sem.at[unit, part_of],
        )

    order = []
    for near in range(chips // 2):
        order += [near, last - near]

    barrier = pltpu.get_barrier_semaphore()
    pl.semaphore_signal(barrier, inc=1, device_id={"fsdp": sibling}, device_id_type=MESH)
    pl.semaphore_signal(barrier, inc=1, device_id={"replica": source}, device_id_type=MESH)

    @pl.when(chip > 0)
    def _():
        pl.semaphore_signal(barrier, inc=1, device_id={"fsdp": left}, device_id_type=MESH)

    @pl.when(chip < last)
    def _():
        pl.semaphore_signal(barrier, inc=1, device_id={"fsdp": right}, device_id_type=MESH)

    @pl.when(next_to_end)
    def _():
        pl.semaphore_signal(
            barrier, inc=1, device_id={"fsdp": outer * 2 + 1 - core}, device_id_type=MESH
        )

    for unit in range(units):
        own_grad(unit).start()
    def needs(target):
        return jnp.logical_or(jnp.logical_not(at_end), chip == target)

    for target in order:

        @pl.when(needs(target))
        def _(target=target):
            own_copy(target).start()

    pl.semaphore_wait(barrier, 4)

    for unit in range(units):
        own_grad(unit).wait()

    @pl.when(at_end)
    def _():
        edge_grad_copy(0).start()
        edge_copy(0, 0).start()
        edge_copy(0, 1).start()

    for unit in range(units):
        sibling_grad(unit).start()
    for target in order:

        @pl.when(needs(target))
        def _(target=target):
            sibling_copy(target).start()

    @pl.when(at_end)
    def _():
        for unit in range(1, units):
            edge_grad_copy(unit).start()
        for rank in range(1, last):
            edge_copy(rank, 0).start()
            edge_copy(rank, 1).start()

    for unit in range(units):
        for copy in load(unit):
            copy.start()

    for unit in range(units):
        sibling_grad(unit).wait_recv()

    def dot(a, b):
        return lax.dot_general(
            a.reshape(-1, a.shape[-1]),
            b.reshape(-1, b.shape[-1]),
            (((0,), (0,)), ((), ())),
            preferred_element_type=jnp.float32,
        )

    def decode(data, factors):
        return data.astype(jnp.int32).astype(jnp.float32) * factors

    def encode(value):
        largest = jnp.max(jnp.abs(value), axis=0, keepdims=True)
        largest = jnp.maximum(largest, TINY)
        code = jnp.round(value * (TOP / largest * (1.0 - 1e-6)))
        return code.astype(jnp.int32).astype(jnp.int16), largest * (1.0 / TOP / (1.0 - 1e-6))

    def multiply(slot, target, rank, unit, with_edge):
        @pl.when(unit == 0)
        def _():
            own_copy(target).wait()
            sibling_copy(target).wait_recv()

        part[slot] = dot(tok[target], grad[unit])

        @pl.when(with_edge)
        def _():
            @pl.when(rank == 0)
            def _():
                edge_grad_arrival(unit).wait_recv()
                pass_copy(unit, core).start()
                pass_copy(unit, 1 - core).wait_recv()

            @pl.when(unit == 0)
            def _():
                edge_arrival(rank, 0).wait_recv()
                edge_arrival(rank, 1).wait_recv()

            part[slot] += dot(edge_tok[rank], edge_grad[unit])

    def forward(way, at, beside_end):
        rank = at // units
        multiply(way, rank if way == 0 else last - rank, rank, at % units, beside_end)

        @pl.when(jnp.logical_not(beside_end))
        def _():
            hop_factor(way, at).wait_recv()
            hop_whole(way, at).wait_recv()
            part[way] += decode(buf[way, at], factor[way, at])

        buf[way, at], factor[way, at] = encode(part[way])
        hop_factor(way, at).start()

        @pl.when(is_late(at))
        def _():
            hop_half(way, at, 0).start()
            hop_half(way, at, 1).start()

        @pl.when(jnp.logical_not(is_late(at)))
        def _():
            hop_whole(way, at).start()

    from_right = chip * units
    from_left = (last - chip) * units
    lag_right = jnp.maximum(last - 1 - chip, 0) * HOP
    lag_left = jnp.maximum(chip - 1, 0) * HOP
    largest_slot = (last - 1) * units - 1

    def finish(unit):
        multiply(2, chip, last - 1, unit, next_to_end)

        for part_of in range(2):
            rows = slice(part_of * half, (part_of + 1) * half)

            for way, begin, there in ((0, from_right, chip < last - 1), (1, from_left, chip > 1)):

                @pl.when(there)
                def _(way=way, begin=begin):
                    at = jnp.minimum(begin + unit, largest_slot)
                    late = is_late(at)
                    if part_of == 0:
                        hop_factor(way, at).wait_recv()

                        @pl.when(jnp.logical_not(late))
                        def _():
                            hop_whole(way, at).wait_recv()

                    @pl.when(late)
                    def _():
                        hop_half(way, at, part_of).wait_recv()

                    part[2, rows] += decode(buf[way, at, rows], factor[way, at])

            if part_of == 0:
                for copy in load(unit):
                    copy.wait()
            moment = 0.9 * moments[unit, rows] + part[2, rows] * scale
            new[unit, rows] = moment
            value = weights[unit, rows].astype(jnp.float32) - 0.05 * moment
            updated[unit, rows] = value
            out_buf[unit, rows], out_factor[unit, part_of] = encode(value)
            for copy in gossip(unit, part_of):
                copy.start()
        new_copy(unit).start()

    begin_finish = jnp.maximum(
        jnp.where(chip < last, from_right + lag_right, 0),
        jnp.where(chip > 0, from_left + lag_left, 0),
    )

    def step(i, carry):
        at_l = i - lag_right
        at_r = i - lag_left
        unit = i - begin_finish

        @pl.when((at_l >= 0) & (at_l < from_right) & (chip < last))
        def _():
            forward(0, at_l, chip == last - 1)

        @pl.when((at_r >= 0) & (at_r < from_left) & (chip > 0))
        def _():
            forward(1, at_r, chip == 1)

        @pl.when((unit >= 0) & (unit < units))
        def _():
            finish(unit)

        return carry

    steps = (last - 1) * max(units, HOP) + units + HOP
    lax.fori_loop(0, steps, step, 0)

    def mix(i, carry):
        unit, part_of = i // 2, i % 2
        for copy in gossip(unit, part_of):
            copy.wait_recv()
        rows = half_rows(part_of)
        theirs = decode(in_buf[unit, rows], in_factor[unit, part_of])
        mixed[unit, rows] = ((updated[unit, rows] + theirs) * 0.5).astype(jnp.bfloat16)
        mixed_copy(unit, part_of).start()
        return carry

    lax.fori_loop(0, 2 * units, mix, 0)

    def drain_way(way, at):
        hop_factor(way, at).wait_send()

        @pl.when(is_late(at))
        def _():
            hop_half(way, at, 0).wait_send()
            hop_half(way, at, 1).wait_send()

        @pl.when(jnp.logical_not(is_late(at)))
        def _():
            hop_whole(way, at).wait_send()

    def drain_left(at, carry):
        drain_way(0, at)
        return carry

    def drain_right(at, carry):
        drain_way(1, at)
        return carry

    lax.fori_loop(0, jnp.where(chip < last, from_right, 0), drain_left, 0)
    lax.fori_loop(0, jnp.where(chip > 0, from_left, 0), drain_right, 0)

    @pl.when(at_end)
    def _():
        for unit in range(units):
            edge_grad_copy(unit).wait_send()
        for rank in range(last):
            edge_copy(rank, 0).wait_send()
            edge_copy(rank, 1).wait_send()

    @pl.when(next_to_end)
    def _():
        for unit in range(units):
            pass_copy(unit, core).wait_send()

    for unit in range(units):
        sibling_grad(unit).wait_send()
    for target in range(chips):

        @pl.when(needs(target))
        def _(target=target):
            sibling_copy(target).wait_send()

    def drain(unit, carry):
        new_copy(unit).wait()
        for part_of in range(2):
            for copy in gossip(unit, part_of):
                copy.wait_send()
            mixed_copy(unit, part_of).wait()
        return carry

    lax.fori_loop(0, units, drain, 0)


def step_with(level, replicas, members, tokens, grads_out, weights, moments):
    chips = members // 2
    last = chips - 1
    held = tokens.shape[0]
    columns = grads_out.shape[1]
    features = weights.shape[1]
    width = min(LANES, columns)
    units = columns // width
    passed = (last - 1) * units
    dma = pltpu.SemaphoreType.DMA
    return pl.pallas_call(
        functools.partial(kernel, replicas, chips, 1 << level, float((held * members) ** -0.5)),
        out_shape=(
            jax.ShapeDtypeStruct(weights.shape, jnp.bfloat16),
            jax.ShapeDtypeStruct(moments.shape, jnp.float32),
        ),
        in_specs=[pl.BlockSpec(memory_space=pl.ANY)] * 4,
        out_specs=[pl.BlockSpec(memory_space=pl.ANY)] * 2,
        scratch_shapes=[
            pltpu.VMEM((chips, 2, held, features), jnp.bfloat16),
            pltpu.VMEM((units, 2, held, width), jnp.bfloat16),
            pltpu.VMEM((last, 2, held, features), jnp.bfloat16),
            pltpu.VMEM((units, 2, held, width), jnp.bfloat16),
            pltpu.VMEM((2, passed, features, width), jnp.int16),
            pltpu.VMEM((2, passed, 1, width), jnp.float32),
            pltpu.VMEM((3, features, width), jnp.float32),
            pltpu.VMEM((units, features, width), jnp.bfloat16),
            pltpu.VMEM((units, features, width), jnp.float32),
            pltpu.VMEM((units, features, width), jnp.float32),
            pltpu.VMEM((units, features, width), jnp.float32),
            pltpu.VMEM((units, features, width), jnp.bfloat16),
            pltpu.VMEM((units, features, width), jnp.int16),
            pltpu.VMEM((units, 2, 1, width), jnp.float32),
            pltpu.VMEM((units, features, width), jnp.int16),
            pltpu.VMEM((units, 2, 1, width), jnp.float32),
            dma((chips,)),
            dma((chips,)),
            dma((chips,)),
            dma((units,)),
            dma((units,)),
            dma((units,)),
            dma((2, units)),
            dma((last, 2)),
            dma((last, 2)),
            dma((units,)),
            dma((units,)),
            dma((units,)),
            dma((units,)),
            dma((2, passed)),
            dma((2, passed)),
            dma((2, passed)),
            dma((2, passed)),
            dma((2, units)),
            dma((2, units)),
            dma((units, 2)),
            dma((units, 2)),
            dma((units, 2)),
            dma((units, 2)),
            dma((units,)),
            dma((units, 2)),
        ],
        compiler_params=pltpu.CompilerParams(
            collective_id=level, has_side_effects=True, vmem_limit_bytes=44 * 1024 * 1024
        ),
        cost_estimate=pl.CostEstimate(
            flops=2 * held * members * features * columns,
            bytes_accessed=2 * tokens.size + 10 * features * columns,
            transcendentals=0,
        ),
    )(tokens, grads_out, weights, moments)


def solution(mesh):
    replicas, members = mesh.shape["replica"], mesh.shape["fsdp"]
    levels = replicas.bit_length() - 1

    def body(tokens, grads_out, weights, moments, step):
        level = step[0] % levels
        branches = [
            functools.partial(step_with, power, replicas, members) for power in range(levels)
        ]
        return lax.switch(level, branches, tokens, grads_out, weights, moments)

    return jax.shard_map(
        body,
        mesh=mesh,
        in_specs=(
            P(("replica", "fsdp"), None),
            P(("replica", "fsdp"), None),
            P("replica", "fsdp", None),
            P("replica", "fsdp", None),
            P(),
        ),
        out_specs=(P("replica", "fsdp", None), P("replica", "fsdp", None)),
        check_vma=False,
    )
```
